128 devices in a mesh: freq: 8 (over z_lo, y), pts: 16 (over z_hi, x, core).
Axes of the slice: x: 4, y: 4, z: 4 (z_hi: 2, z_lo: 2; z = z_hi * 2 + z_lo), core: 2. Of those that a mesh axis runs over, the one named last changes fastest.
Arguments:
- orbitals: bfloat16 [16384, 512], P('pts'), may hold values from -6 to 6
- energies: float32 [512], replicated, may hold values from -1 to 1
- freq_nodes: float32 [16], P('freq'), may hold values from 0.05 to 4
- weights_q: float32 [16], P('freq'), may hold values from 0.02 to 0.2
- screened: bfloat16 [8192, 16, 4096], P('pts', 'freq'), may hold values from -0.0014648438 to 0.0014648438
- tile_rows: int32 [8192], P('pts'), may hold values from 0 to 15
- tile_cols: int32 [8192], P('pts'), may hold values from 0 to 255, as said below
- tile_count: int32 [16], P('pts'), may hold values from 64 to 512, as said below
Outputs:
- sigma: float32 [512], replicated
The draws below stay inside these ranges and needn't reach their ends.
Inputs may be any that keep to these rules, and one draw needn't show every extreme that they name: Each group's live slots are its first tile_count slots; one group has exactly 512. `tile_cols`: A slot's column tile lies within 16 tiles of its global row tile.
All inputs are finite; a program needn't handle non-finite values.
Results may differ from the reference program's by a relative error of at most 0.0045.
Values may be sent and summed in bfloat16 or wider, within the bound.
No kernel may reach another device: no remote copies, remote signals or barrier semaphores. Data moves between devices by JAX's collectives and lax.ppermute only.
A program may use at most 64 MiB of HBM per device.

```python
import math
import jax
import jax.numpy as jnp
from jax import lax

ORBS = 512
TILE = 64
TT = 4096
ROW_TILES = 16
POINTS = 16384
COL_TILES = 256
TMAX = 512
TILES = 8192
FREQS = 16


def tile_helper(key):
    groups = TILES // TMAX
    base = jax.random.fold_in(key, 7)
    key_counts, key_peak, key_rows, key_shift = jax.random.split(base, 4)
    counts = jax.random.randint(key_counts, (groups,), TMAX // 8, TMAX // 2 + 1)
    peak = jax.random.randint(key_peak, (), 0, groups)
    counts = jnp.where(jnp.arange(groups) == peak, TMAX, counts).astype(jnp.int32)
    rows_drawn = jax.random.randint(key_rows, (TILES,), 0, ROW_TILES).astype(jnp.int32)
    shifts = jax.random.randint(key_shift, (TILES,), -ROW_TILES, ROW_TILES + 1)
    owner = jnp.arange(TILES) // TMAX
    columns = jnp.clip(owner * ROW_TILES + rows_drawn + shifts, 0, COL_TILES - 1).astype(jnp.int32)
    return (counts, rows_drawn, columns)


def draw_tile_count(key, part):
    return tile_helper(key)[0]


def draw_tile_rows(key, part):
    return tile_helper(key)[1]


def draw_tile_cols(key, part):
    return tile_helper(key)[2]


def block_scale(own_key, dims, pieces, smallest, largest):
    def one(axis_at, blocks):
        draws = jax.random.uniform(jax.random.fold_in(jax.random.fold_in(own_key, 6), axis_at), (blocks,), jnp.float32, smallest / len(pieces), largest / len(pieces))
        return jnp.repeat(jnp.exp(draws), dims[axis_at] // blocks).reshape((-1,) + (1,) * (len(dims) - axis_at - 1))

    loudness = one(*pieces[0])
    for cut in pieces[1:]:
        loudness = loudness * one(*cut)
    return loudness


def scatter_about(stream_key, dims, scale, bound, cuts=(), held_as=jnp.bfloat16):
    entries = jax.random.normal(stream_key, dims, jnp.float32) * scale
    if len(cuts) > 0:
        entries = block_scale(stream_key, dims, cuts, -0.22, 0.18) * entries
    return jnp.clip(entries, min=-bound, max=bound).astype(held_as)


def setup_inputs(seed: int = 0) -> dict:
    key_of = jax.random.split(jax.random.key(seed), 9)
    orbitals = scatter_about(key_of[0], (POINTS, ORBS), 1.0, 6.0, ((0, 16),))
    energies = jnp.clip(jax.random.uniform(key_of[1], (ORBS,), jnp.float32, -1.0, 1.0), -1.0, 1.0)
    freq_nodes = jnp.clip(jnp.exp(math.log(4.0) - 4.3820266 * jax.random.uniform(key_of[2], (FREQS,), jnp.float32) ** block_scale(key_of[2], (FREQS,), ((0, 8),), -0.2, 0.2)), 0.05, 4.0)
    weights_q = jnp.clip(jnp.exp(math.log(0.2) - 2.3025851 * jax.random.uniform(key_of[3], (FREQS,), jnp.float32) ** block_scale(key_of[3], (FREQS,), ((0, 8),), -0.2, 0.2)), 0.02, 0.2)
    screened = scatter_about(key_of[4], (TILES, FREQS, TT), (50.0 / (TILE * (TILES * FREQS * ORBS) ** 0.5)), 0.0014648438, ((0, 16), (1, 8)))
    tile_rows = draw_tile_rows(jax.random.fold_in(key_of[8], 71), 0)
    tile_cols = draw_tile_cols(jax.random.fold_in(key_of[8], 71), 0)
    tile_count = draw_tile_count(jax.random.fold_in(key_of[8], 71), 0)
    return dict(orbitals=orbitals, energies=energies, freq_nodes=freq_nodes, weights_q=weights_q, screened=screened, tile_rows=tile_rows, tile_cols=tile_cols, tile_count=tile_count)


def reference(orbitals, energies, freq_nodes, weights_q, screened, tile_rows, tile_cols, tile_count):
    table = orbitals.reshape(COL_TILES, TILE, ORBS)
    slots = jnp.arange(TILES, dtype=jnp.int32)
    group = (slots // TMAX).astype(jnp.int32)
    alive = ((slots - group * TMAX) < tile_count[group]).astype(jnp.float32)
    global_rows = (group * ROW_TILES + tile_rows).astype(jnp.int32)
    green_weight = energies[None, :] / (energies[None, :] ** 2 + freq_nodes[:, None] ** 2)
    block_size = 16
    block_count = TILES // block_size

    def advance(running, block_id):
        chosen = (block_id * block_size + jnp.arange(block_size, dtype=jnp.int32)).astype(jnp.int32)
        left = table[global_rows[chosen]].astype(jnp.float32)
        right = table[tile_cols[chosen]].astype(jnp.float32)
        tiles = screened[chosen].astype(jnp.float32).reshape(block_size, FREQS, TILE, TILE)
        scaled = (right[:, None, :, :] * green_weight[None, :, None, :]).astype(jnp.bfloat16)
        scaled = lax.optimization_barrier(scaled).astype(jnp.float32)
        green = jnp.einsum("rim,rfjm->rfij", left, scaled, precision=lax.Precision.HIGHEST)
        product = (green * tiles).astype(jnp.bfloat16)
        product = lax.optimization_barrier(product).astype(jnp.float32)
        image = jnp.einsum("rfij,rjm->rfim", product, right, precision=lax.Precision.HIGHEST)
        terms = jnp.sum(image * left[:, None, :, :], axis=2)
        terms = terms * alive[chosen][:, None, None]
        weighted = jnp.sum(terms * weights_q[None, :, None], axis=(0, 1))
        return running + weighted, None

    total, _ = lax.scan(advance, jnp.zeros((ORBS,), jnp.float32), jnp.arange(block_count, dtype=jnp.int32))
    return -total
```

```python
import jax
import jax.numpy as jnp
from jax import lax
from jax.experimental import pallas as pl
from jax.experimental.pallas import tpu as pltpu
from jax.sharding import PartitionSpec as P

ORBS = 512
TILE = 64
HALF = 32
BAND = 16
BLOCK = 4
SPAN = BLOCK * TILE
BLOCKS = BAND // BLOCK
CHUNK = 64

F32 = jnp.float32
BF16 = jnp.bfloat16


def weight_row(energies, node):
    return energies / (energies * energies + node * node)


def scale_into(scaled, points, energies_ref, nodes_ref):
    for f in range(2):
        weight = weight_row(energies_ref[...], nodes_ref[f])
        scaled[f] = (points[...].astype(F32) * weight).astype(BF16)


def block_terms(rows, cols_scaled, cols, w_of, ratio):
    dims = (((1,), (1,)), ((), ()))
    g0 = lax.dot_general(rows, cols_scaled(0), dims, preferred_element_type=F32)
    g1 = lax.dot_general(rows, cols_scaled(1), dims, preferred_element_type=F32)
    product = g0 * w_of(0).astype(F32) + ratio * (g1 * w_of(1).astype(F32))
    image = jnp.dot(product.astype(BF16), cols(), preferred_element_type=F32)
    return jnp.sum(image * rows.astype(F32), axis=0, keepdims=True)


def own_kernel(
    count_ref,
    rows_ref,
    cols_ref,
    nodes_ref,
    weights_ref,
    orb_ref,
    energies_ref,
    screened_ref,
    sigma_ref,
    perm_ref,
    halo_ref,
    raw,
    dense,
    sorted_w,
    scaled,
    wide,
    raw_sem,
    out_sem,
):
    slots = screened_ref.shape[0]
    chunks = slots // CHUNK
    count = count_ref[0]
    first = (lax.axis_index("pts") - 1) * BAND

    def fetch(k):
        part = pl.ds(k * CHUNK, CHUNK)
        return pltpu.make_async_copy(screened_ref.at[part], raw.at[part], raw_sem.at[k])

    for k in range(chunks):

        @pl.when(k * CHUNK < count)
        def _():
            fetch(k).start()

    for q in range(ORBS // 128):
        lanes = pl.ds(q * 128, 128)
        wide[q] = orb_ref[:, lanes].astype(F32)
        for b in range(BLOCKS):
            for h in range(2):
                perm_ref[pl.ds(b * SPAN + h * SPAN // 2, SPAN // 2), lanes] = wide[
                    q, pl.ds(b * SPAN + h, SPAN // 2, stride=2), :
                ].astype(BF16)
    scale_into(scaled, orb_ref, energies_ref, nodes_ref)

    def clear(r, carry):
        dense[:, r] = jnp.zeros(dense.shape[:1] + dense.shape[2:], F32)
        return carry

    lax.fori_loop(0, BAND, clear, 0)

    def place(s):
        return rows_ref[s], cols_ref[s] - first

    def values(s):
        return raw[s].astype(F32).reshape(2, HALF, 2 * TILE)

    def scatter(s):
        r, c = place(s)
        dense[:, r, c] = dense[:, r, c] + values(s)

    def scatter_two(s):
        r0, c0 = place(s)
        r1, c1 = place(s + 1)
        same = ((r0 == r1) & (c0 == c1)).astype(jnp.int32).astype(F32)
        x0 = values(s)
        x1 = values(s + 1)
        old0 = dense[:, r0, c0]
        old1 = dense[:, r1, c1]
        dense[:, r0, c0] = old0 + x0
        dense[:, r1, c1] = old1 + (x1 + same * x0)

    for k in range(chunks):

        @pl.when(k * CHUNK < count)
        def _():
            fetch(k).wait()
            here = jnp.minimum(count - k * CHUNK, CHUNK)

            def two(i, carry):
                scatter_two(k * CHUNK + 2 * i)
                return carry

            lax.fori_loop(0, here // 2, two, 0)

            @pl.when(here % 2 == 1)
            def _():
                scatter(k * CHUNK + here - 1)

    low = lax.broadcasted_iota(jnp.int32, (SPAN // 2, 2 * TILE), 1) < TILE

    def arrange(side, f, b, pair):
        parts = []
        for d in range(2):
            c = side * BAND + 2 * pair + d
            parts.append(dense[f, pl.ds(b * BLOCK, BLOCK), c].reshape(SPAN // 2, 2 * TILE))
        v0, v1 = parts
        even = jnp.where(low, v0, pltpu.roll(v1, TILE, 1))
        odd = jnp.where(low, pltpu.roll(v0, TILE, 1), v1)
        lanes = pl.ds(pair * 2 * TILE, 2 * TILE)
        sorted_w[side, f, pl.ds(b * SPAN, SPAN // 2), lanes] = even.astype(BF16)
        sorted_w[side, f, pl.ds(b * SPAN + SPAN // 2, SPAN // 2), lanes] = odd.astype(BF16)

    def arrange_block(side, b, c):
        for f in range(2):
            for pair in range(2 * c, 2 * c + 2):
                arrange(side, f, b, pair)

    outs = [
        pltpu.make_async_copy(sorted_w.at[2 * k], halo_ref.at[k], out_sem.at[k]) for k in range(2)
    ]
    for b in range(BLOCKS):
        for c in range(BLOCKS):
            if c >= b:
                arrange_block(0, b, c)
            if c <= b:
                arrange_block(2, b, c)
    for copy in outs:
        copy.start()
    ratio = weights_ref[1] / weights_ref[0]
    total = jnp.zeros((1, ORBS), F32)
    for b in range(BLOCKS):
        for c in range(BLOCKS):
            arrange_block(1, b, c)
        total += block_terms(
            perm_ref[pl.ds(b * SPAN, SPAN), :],
            lambda f: scaled[f],
            lambda: orb_ref[...],
            lambda f: sorted_w[1, f, pl.ds(b * SPAN, SPAN), :],
            ratio,
        )
    sigma_ref[...] = -weights_ref[0] * total
    for copy in outs:
        copy.wait()


def own_part(count, rows, cols, nodes, weights, orbitals, energies, screened):
    points = orbitals.shape[0]
    smem = pl.BlockSpec(memory_space=pltpu.SMEM)
    vmem = pl.BlockSpec(memory_space=pltpu.VMEM)
    hbm = pl.BlockSpec(memory_space=pl.ANY)
    return pl.pallas_call(
        own_kernel,
        out_shape=(
            jax.ShapeDtypeStruct((1, ORBS), F32),
            jax.ShapeDtypeStruct((points, ORBS), BF16),
            jax.ShapeDtypeStruct((2, 2, points, points), BF16),
        ),
        in_specs=[smem] * 5 + [vmem, vmem, hbm],
        out_specs=(vmem, vmem, hbm),
        scratch_shapes=[
            pltpu.VMEM(screened.shape, BF16),
            pltpu.VMEM((2, BAND, 3 * BAND, HALF, 2 * TILE), F32),
            pltpu.VMEM((3, 2, points, points), BF16),
            pltpu.VMEM((2, points, ORBS), BF16),
            pltpu.VMEM((ORBS // 128, points, 128), F32),
            pltpu.SemaphoreType.DMA((screened.shape[0] // CHUNK,)),
            pltpu.SemaphoreType.DMA((2,)),
        ],
        compiler_params=pltpu.CompilerParams(vmem_limit_bytes=58 << 20),
    )(count, rows, cols, nodes, weights, orbitals, energies, screened)


def halo_kernel(
    side_ref,
    nodes_ref,
    weights_ref,
    perm_ref,
    orb_ref,
    energies_ref,
    sigma_in,
    halo_ref,
    sigma_ref,
    tiles,
    scaled,
    sem,
):
    side = side_ref[0]
    copy = pltpu.make_async_copy(halo_ref.at[side], tiles, sem)
    copy.start()
    scale_into(scaled, orb_ref, energies_ref, nodes_ref)
    copy.wait()
    ratio = weights_ref[1] / weights_ref[0]
    total = jnp.zeros((1, ORBS), F32)
    for t in range(BLOCKS):
        width = (BLOCKS - t) * SPAN
        b = t + side * (BLOCKS - 1 - 2 * t)
        rows = pl.ds(pl.multiple_of(b * SPAN, SPAN), SPAN)
        lead = (1 - side) * t
        cols = pl.ds(pl.multiple_of(lead * SPAN, SPAN), width)
        total += block_terms(
            perm_ref[rows, :],
            lambda f: scaled[f, cols, :],
            lambda: orb_ref[cols, :],
            lambda f: tiles[f, rows, cols],
            ratio,
        )
    sigma_ref[...] = sigma_in[...] - weights_ref[0] * total


def halo_part(side, nodes, weights, perm, orbitals, energies, sigma, halo):
    points = orbitals.shape[0]
    smem = pl.BlockSpec(memory_space=pltpu.SMEM)
    vmem = pl.BlockSpec(memory_space=pltpu.VMEM)
    hbm = pl.BlockSpec(memory_space=pl.ANY)
    return pl.pallas_call(
        halo_kernel,
        out_shape=jax.ShapeDtypeStruct((1, ORBS), F32),
        in_specs=[smem] * 3 + [vmem] * 4 + [hbm],
        out_specs=vmem,
        scratch_shapes=[
            pltpu.VMEM(halo.shape[1:], BF16),
            pltpu.VMEM((2, points, ORBS), BF16),
            pltpu.SemaphoreType.DMA,
        ],
        compiler_params=pltpu.CompilerParams(vmem_limit_bytes=58 << 20),
    )(side, nodes, weights, perm, orbitals, energies, sigma, halo)


AXES = ("freq", "pts")


def device(f, p):
    return f * 16 + p


def inner_pairs():
    return [(device(f, p), device(f, p ^ 1)) for f in range(8) for p in range(16)]


def outer_pairs():
    pairs = []
    for f in range(8):
        for p in range(1, 15, 2):
            to = device(f ^ 4 if p == 7 else f, p + 1)
            pairs += [(device(f, p), to), (to, device(f, p))]
    return pairs


def total_over_devices(x):
    for mask in (1, 2, 6, 64, 72, 16, 48):
        x = x + lax.ppermute(x, AXES, [(i, i ^ mask) for i in range(128)])
    return x


def body(orbitals, energies, freq_nodes, weights_q, screened, tile_rows, tile_cols, tile_count):
    position = lax.axis_index("pts")
    outer = lax.ppermute(orbitals, AXES, outer_pairs())
    inner = lax.ppermute(orbitals, AXES, inner_pairs())
    energies = energies[None, :]
    sigma, perm, halo = own_part(
        tile_count, tile_rows, tile_cols, freq_nodes, weights_q, orbitals, energies, screened
    )
    odd = (position % 2).astype(jnp.int32)
    for side, points in ((1 - odd, inner), (odd, outer)):
        sigma = halo_part(
            side[None], freq_nodes, weights_q, perm, points, energies, sigma, halo
        )
    return total_over_devices(sigma[0])


def solution(mesh):
    placed = (
        P("pts", None),
        P(),
        P("freq"),
        P("freq"),
        P("pts", "freq", None),
        P("pts"),
        P("pts"),
        P("pts"),
    )
    return jax.shard_map(body, mesh=mesh, in_specs=placed, out_specs=P(), check_vma=False)
```

```python
import jax
import jax.numpy as jnp
from jax import lax
from jax.experimental import pallas as pl
from jax.experimental.pallas import tpu as pltpu
from jax.sharding import PartitionSpec as P

ORBS = 512
TILE = 64
HALF = 32
BAND = 16
BLOCK = 4
SPAN = BLOCK * TILE
BLOCKS = BAND // BLOCK
UNROLL = 4
CHUNK = 64

F32 = jnp.float32
BF16 = jnp.bfloat16


def weight_row(energies, node):
    return energies / (energies * energies + node * node)


def scale_into(scaled, points, energies_ref, nodes_ref):
    for f in range(2):
        weight = weight_row(energies_ref[...], nodes_ref[f])
        scaled[f] = (points[...].astype(F32) * weight).astype(BF16)


def block_terms(rows, cols_scaled, cols, w_of, ratio):
    dims = (((1,), (1,)), ((), ()))
    g0 = lax.dot_general(rows, cols_scaled(0), dims, preferred_element_type=F32)
    g1 = lax.dot_general(rows, cols_scaled(1), dims, preferred_element_type=F32)
    product = g0 * w_of(0).astype(F32) + ratio * (g1 * w_of(1).astype(F32))
    image = jnp.dot(product.astype(BF16), cols(), preferred_element_type=F32)
    return jnp.sum(image * rows.astype(F32), axis=0, keepdims=True)


def own_kernel(
    count_ref,
    rows_ref,
    cols_ref,
    nodes_ref,
    weights_ref,
    orb_ref,
    energies_ref,
    screened_ref,
    sigma_ref,
    perm,
    halo,
    points,
    raw,
    dense,
    own_w,
    scaled,
    wide,
    raw_sem,
    orb_sem,
):
    slots = screened_ref.shape[0]
    chunks = slots // CHUNK
    count = count_ref[0]
    first = (lax.axis_index("pts") - 1) * BAND

    def fetch(k):
        part = pl.ds(k * CHUNK, CHUNK)
        return pltpu.make_async_copy(screened_ref.at[part], raw.at[part], raw_sem.at[k])

    bring = pltpu.make_async_copy(orb_ref, points, orb_sem)
    bring.start()
    for k in range(chunks):

        @pl.when(k * CHUNK < count)
        def _():
            fetch(k).start()

    for b in range(BLOCKS):

        def clear(r, carry):
            for c in range(b * BLOCK, b * BLOCK + 2 * BAND + BLOCK):
                dense[r, c] = jnp.zeros(dense.shape[2:], F32)
            return carry

        lax.fori_loop(b * BLOCK, (b + 1) * BLOCK, clear, 0)
    bring.wait()

    for q in range(ORBS // 128):
        lanes = pl.ds(q * 128, 128)
        wide[q] = points[:, lanes].astype(F32)
        for b in range(BLOCKS):
            for h in range(2):
                perm[pl.ds(b * SPAN + h * SPAN // 2, SPAN // 2), lanes] = wide[
                    q, pl.ds(b * SPAN + h, SPAN // 2, stride=2), :
                ].astype(BF16)
    scale_into(scaled, points, energies_ref, nodes_ref)

    def place(s):
        return rows_ref[s], cols_ref[s] - first

    def scatter(s, carry):
        r, c = place(s)
        dense[r, c] = dense[r, c] + raw[s].astype(F32)
        return carry

    for k in range(chunks):

        @pl.when(k * CHUNK < count)
        def _():
            fetch(k).wait()
            here = jnp.minimum(count - k * CHUNK, CHUNK)

            def several(i, carry):
                for d in range(UNROLL):
                    scatter(k * CHUNK + i * UNROLL + d, 0)
                return carry

            whole = here // UNROLL
            lax.fori_loop(0, whole, several, 0)
            lax.fori_loop(k * CHUNK + whole * UNROLL, k * CHUNK + here, scatter, 0)

    low = lax.broadcasted_iota(jnp.int32, (SPAN // 2, 2 * TILE), 1) < TILE

    def arrange(side, f, b, pair):
        to_b = BLOCKS - 1 - b if side == 0 else b
        to_pair = (BLOCKS - 1 - pair // 2) * 2 + pair % 2 if side == 0 else pair
        parts = []
        for d in range(2):
            c = side * BAND + 2 * pair + d
            parts.append(dense[pl.ds(b * BLOCK, BLOCK), c, f, :].reshape(SPAN // 2, 2 * TILE))
        v0, v1 = parts
        even = jnp.where(low, v0, pltpu.roll(v1, TILE, 1))
        odd = jnp.where(low, pltpu.roll(v0, TILE, 1), v1)
        lanes = pl.ds(to_pair * 2 * TILE, 2 * TILE)
        to = own_w.at[f] if side == 1 else halo.at[side // 2, f]
        to[pl.ds(to_b * SPAN, SPAN // 2), lanes] = even.astype(BF16)
        to[pl.ds(to_b * SPAN + SPAN // 2, SPAN // 2), lanes] = odd.astype(BF16)

    def arrange_block(side, b, c):
        for f in range(2):
            for pair in range(2 * c, 2 * c + 2):
                arrange(side, f, b, pair)

    for b in range(BLOCKS):
        for c in range(BLOCKS):
            if c >= b:
                arrange_block(0, b, c)
            if c <= b:
                arrange_block(2, b, c)
    ratio = weights_ref[1] / weights_ref[0]
    total = jnp.zeros((1, ORBS), F32)
    for b in range(BLOCKS):
        for c in range(BLOCKS):
            arrange_block(1, b, c)
        total += block_terms(
            perm[pl.ds(b * SPAN, SPAN), :],
            lambda f: scaled[f],
            lambda: points[...],
            lambda f: own_w[f, pl.ds(b * SPAN, SPAN), :],
            ratio,
        )
    sigma_ref[...] = -weights_ref[0] * total


def own_part(count, rows, cols, nodes, weights, orbitals, energies, screened):
    points = orbitals.shape[0]
    smem = pl.BlockSpec(memory_space=pltpu.SMEM)
    vmem = pl.BlockSpec(memory_space=pltpu.VMEM)
    hbm = pl.BlockSpec(memory_space=pl.ANY)
    return pl.pallas_call(
        own_kernel,
        out_shape=(
            pltpu.VMEM((1, ORBS), F32),
            pltpu.VMEM((points, ORBS), BF16),
            pltpu.VMEM((2, 2, points, points), BF16),
        ),
        in_specs=[smem] * 5 + [hbm, vmem, hbm],
        out_specs=(vmem, vmem, vmem),
        scratch_shapes=[
            pltpu.VMEM((points, ORBS), BF16),
            pltpu.VMEM(screened.shape, BF16),
            pltpu.VMEM((BAND, 3 * BAND, 2, TILE * TILE), F32),
            pltpu.VMEM((2, points, points), BF16),
            pltpu.VMEM((2, points, ORBS), BF16),
            pltpu.VMEM((ORBS // 128, points, 128), F32),
            pltpu.SemaphoreType.DMA((screened.shape[0] // CHUNK,)),
            pltpu.SemaphoreType.DMA,
        ],
        compiler_params=pltpu.CompilerParams(vmem_limit_bytes=46 << 20),
    )(count, rows, cols, nodes, weights, orbitals, energies, screened)


def halo_kernel(
    side_ref,
    nodes_ref,
    weights_ref,
    energies_ref,
    sigma_in,
    perm_ref,
    orb_ref,
    halo_ref,
    sigma_ref,
    points,
    scaled,
):
    side = side_ref[0]
    ratio = weights_ref[1] / weights_ref[0]
    total = jnp.zeros((1, ORBS), F32)
    for u in range(BLOCKS):
        block = (1 - side) * (BLOCKS - 1 - u) + side * u
        from_rows = pl.ds(pl.multiple_of(block * SPAN, SPAN), SPAN)
        rows = pl.ds(u * SPAN, SPAN)
        cols = pl.ds(0, (u + 1) * SPAN)
        points[rows, :] = orb_ref[from_rows, :]
        for f in range(2):
            weight = weight_row(energies_ref[...], nodes_ref[f])
            scaled[f, rows] = (points[rows, :].astype(F32) * weight).astype(BF16)
        total += block_terms(
            perm_ref[from_rows, :],
            lambda f: scaled[f, cols, :],
            lambda: points[cols, :],
            lambda f: halo_ref[side, f, rows, cols],
            ratio,
        )
    sigma_ref[...] = sigma_in[...] - weights_ref[0] * total


def halo_part(side, nodes, weights, perm, orbitals, energies, sigma, halo):
    points = orbitals.shape[0]
    smem = pl.BlockSpec(memory_space=pltpu.SMEM)
    vmem = pl.BlockSpec(memory_space=pltpu.VMEM)
    return pl.pallas_call(
        halo_kernel,
        out_shape=pltpu.VMEM((1, ORBS), F32),
        in_specs=[smem] * 3 + [vmem] * 5,
        out_specs=vmem,
        scratch_shapes=[
            pltpu.VMEM((points, ORBS), BF16),
            pltpu.VMEM((2, points, ORBS), BF16),
        ],
        compiler_params=pltpu.CompilerParams(vmem_limit_bytes=16 << 20),
    )(
        side,
        nodes,
        weights,
        energies,
        pltpu.with_memory_space_constraint(sigma, pltpu.VMEM),
        pltpu.with_memory_space_constraint(perm, pltpu.VMEM),
        pltpu.with_memory_space_constraint(orbitals, pltpu.VMEM),
        pltpu.with_memory_space_constraint(halo, pltpu.VMEM),
    )


AXES = ("freq", "pts")


def device(f, p):
    return f * 16 + p


def inner_pairs():
    return [(device(f, p), device(f, p ^ 1)) for f in range(8) for p in range(16)]


def outer_pairs():
    pairs = []
    for f in range(8):
        for p in range(1, 15, 2):
            to = device(f ^ 4 if p == 7 else f, p + 1)
            pairs += [(device(f, p), to), (to, device(f, p))]
    return pairs


def total_over_devices(x):
    for mask in (1, 2, 6, 64, 72, 16, 48):
        x = x + lax.ppermute(x, AXES, [(i, i ^ mask) for i in range(128)])
    return x


def body(orbitals, energies, freq_nodes, weights_q, screened, tile_rows, tile_cols, tile_count):
    position = lax.axis_index("pts")
    outer = lax.ppermute(orbitals, AXES, outer_pairs())
    inner = lax.ppermute(orbitals, AXES, inner_pairs())
    energies = energies[None, :]
    sigma, perm, halo = own_part(
        tile_count, tile_rows, tile_cols, freq_nodes, weights_q, orbitals, energies, screened
    )
    odd = (position % 2).astype(jnp.int32)
    for side, points in ((1 - odd, inner), (odd, outer)):
        sigma = halo_part(
            side[None], freq_nodes, weights_q, perm, points, energies, sigma, halo
        )
    return total_over_devices(sigma[0])


def solution(mesh):
    placed = (
        P("pts", None),
        P(),
        P("freq"),
        P("freq"),
        P("pts", "freq", None),
        P("pts"),
        P("pts"),
        P("pts"),
    )
    return jax.shard_map(body, mesh=mesh, in_specs=placed, out_specs=P(), check_vma=False)
```

```python
import jax
import jax.numpy as jnp
from jax import lax
from jax.experimental import pallas as pl
from jax.experimental.pallas import tpu as pltpu
from jax.sharding import PartitionSpec as P

ORBS = 512
TILE = 64
HALF = 32
BAND = 16
BLOCK = 4
SPAN = BLOCK * TILE
BLOCKS = BAND // BLOCK
UNROLL = 4
CHUNK = 64

F32 = jnp.float32
BF16 = jnp.bfloat16


def weight_row(energies, node):
    return energies / (energies * energies + node * node)


def block_terms(rows, cols_scaled, cols, w_of, ratio):
    dims = (((1,), (1,)), ((), ()))
    g0 = lax.dot_general(rows, cols_scaled(0), dims, preferred_element_type=F32)
    g1 = lax.dot_general(rows, cols_scaled(1), dims, preferred_element_type=F32)
    product = g0 * w_of(0).astype(F32) + ratio * (g1 * w_of(1).astype(F32))
    image = jnp.dot(product.astype(BF16), cols(), preferred_element_type=F32)
    return jnp.sum(image * rows.astype(F32), axis=0, keepdims=True)


def own_kernel(
    count_ref,
    rows_ref,
    cols_ref,
    nodes_ref,
    weights_ref,
    orb_ref,
    energies_ref,
    screened_ref,
    sigma_ref,
    perm,
    halo,
    points,
    raw,
    dense,
    own_w,
    scaled,
    wide,
    raw_sem,
    orb_sem,
):
    slots = screened_ref.shape[0]
    chunks = slots // CHUNK
    count = count_ref[0]
    first = (lax.axis_index("pts") - 1) * BAND

    def fetch(k):
        part = pl.ds(k * CHUNK, CHUNK)
        return pltpu.make_async_copy(screened_ref.at[part], raw.at[part], raw_sem.at[k])

    bring = pltpu.make_async_copy(orb_ref, points, orb_sem)
    bring.start()
    for k in range(chunks):

        @pl.when(k * CHUNK < count)
        def _():
            fetch(k).start()

    for b in range(BLOCKS):

        def clear(r, carry):
            for c in range(b * BLOCK, b * BLOCK + 2 * BAND + BLOCK):
                dense[r, c] = jnp.zeros(dense.shape[2:], F32)
            return carry

        lax.fori_loop(b * BLOCK, (b + 1) * BLOCK, clear, 0)
    bring.wait()

    for q in range(ORBS // 128):
        lanes = pl.ds(q * 128, 128)
        values = points[:, lanes].astype(F32)
        wide[q] = values
        for f in range(2):
            weight = weight_row(energies_ref[:, lanes], nodes_ref[f])
            scaled[f, :, lanes] = (values * weight).astype(BF16)
        for b in range(BLOCKS):
            for h in range(2):
                part = wide[q, pl.ds(b * SPAN + h, SPAN // 2, stride=2), :]
                perm[pl.ds(b * SPAN + h * SPAN // 2, SPAN // 2), lanes] = part.astype(BF16)

    def place(s):
        return rows_ref[s], cols_ref[s] - first

    def scatter(s, carry):
        r, c = place(s)
        dense[r, c] = dense[r, c] + raw[s].astype(F32)
        return carry

    for k in range(chunks):

        @pl.when(k * CHUNK < count)
        def _():
            fetch(k).wait()
            here = jnp.minimum(count - k * CHUNK, CHUNK)

            def several(i, carry):
                for d in range(UNROLL):
                    scatter(k * CHUNK + i * UNROLL + d, 0)
                return carry

            whole = here // UNROLL
            lax.fori_loop(0, whole, several, 0)
            lax.fori_loop(k * CHUNK + whole * UNROLL, k * CHUNK + here, scatter, 0)

    low = lax.broadcasted_iota(jnp.int32, (SPAN // 2, 2 * TILE), 1) < TILE

    def arrange(side, f, b, pair):
        to_b = BLOCKS - 1 - b if side == 0 else b
        to_pair = (BLOCKS - 1 - pair // 2) * 2 + pair % 2 if side == 0 else pair
        parts = []
        for d in range(2):
            c = side * BAND + 2 * pair + d
            parts.append(dense[pl.ds(b * BLOCK, BLOCK), c, f, :].reshape(SPAN // 2, 2 * TILE))
        v0, v1 = parts
        even = jnp.where(low, v0, pltpu.roll(v1, TILE, 1))
        odd = jnp.where(low, pltpu.roll(v0, TILE, 1), v1)
        lanes = pl.ds(to_pair * 2 * TILE, 2 * TILE)
        to = own_w.at[f] if side == 1 else halo.at[side // 2, f]
        to[pl.ds(to_b * SPAN, SPAN // 2), lanes] = even.astype(BF16)
        to[pl.ds(to_b * SPAN + SPAN // 2, SPAN // 2), lanes] = odd.astype(BF16)

    def arrange_block(side, b, c):
        for f in range(2):
            for pair in range(2 * c, 2 * c + 2):
                arrange(side, f, b, pair)

    for b in range(BLOCKS):
        for c in range(BLOCKS):
            if c >= b:
                arrange_block(0, b, c)
            if c <= b:
                arrange_block(2, b, c)
    ratio = weights_ref[1] / weights_ref[0]
    total = jnp.zeros((1, ORBS), F32)
    for b in range(BLOCKS):
        for c in range(BLOCKS):
            arrange_block(1, b, c)
        total += block_terms(
            perm[pl.ds(b * SPAN, SPAN), :],
            lambda f: scaled[f],
            lambda: points[...],
            lambda f: own_w[f, pl.ds(b * SPAN, SPAN), :],
            ratio,
        )
    sigma_ref[...] = -weights_ref[0] * total


def own_part(count, rows, cols, nodes, weights, orbitals, energies, screened):
    points = orbitals.shape[0]
    smem = pl.BlockSpec(memory_space=pltpu.SMEM)
    vmem = pl.BlockSpec(memory_space=pltpu.VMEM)
    hbm = pl.BlockSpec(memory_space=pl.ANY)
    return pl.pallas_call(
        own_kernel,
        out_shape=(
            pltpu.VMEM((1, ORBS), F32),
            pltpu.VMEM((points, ORBS), BF16),
            pltpu.VMEM((2, 2, points, points), BF16),
        ),
        in_specs=[smem] * 5 + [hbm, vmem, hbm],
        out_specs=(vmem, vmem, vmem),
        scratch_shapes=[
            pltpu.VMEM((points, ORBS), BF16),
            pltpu.VMEM(screened.shape, BF16),
            pltpu.VMEM((BAND, 3 * BAND, 2, TILE * TILE), F32),
            pltpu.VMEM((2, points, points), BF16),
            pltpu.VMEM((2, points, ORBS), BF16),
            pltpu.VMEM((ORBS // 128, points, 128), F32),
            pltpu.SemaphoreType.DMA((screened.shape[0] // CHUNK,)),
            pltpu.SemaphoreType.DMA,
        ],
        compiler_params=pltpu.CompilerParams(vmem_limit_bytes=46 << 20),
    )(count, rows, cols, nodes, weights, orbitals, energies, screened)


def halo_kernel(
    side_ref,
    nodes_ref,
    weights_ref,
    energies_ref,
    sigma_in,
    perm_ref,
    orb_ref,
    halo_ref,
    sigma_ref,
    points,
    scaled,
):
    side = side_ref[0]
    ratio = weights_ref[1] / weights_ref[0]
    total = jnp.zeros((1, ORBS), F32)
    for u in range(BLOCKS):
        block = (1 - side) * (BLOCKS - 1 - u) + side * u
        from_rows = pl.ds(pl.multiple_of(block * SPAN, SPAN), SPAN)
        rows = pl.ds(u * SPAN, SPAN)
        cols = pl.ds(0, (u + 1) * SPAN)
        points[rows, :] = orb_ref[from_rows, :]
        for f in range(2):
            weight = weight_row(energies_ref[...], nodes_ref[f])
            scaled[f, rows] = (points[rows, :].astype(F32) * weight).astype(BF16)
        total += block_terms(
            perm_ref[from_rows, :],
            lambda f: scaled[f, cols, :],
            lambda: points[cols, :],
            lambda f: halo_ref[side, f, rows, cols],
            ratio,
        )
    sigma_ref[...] = sigma_in[...] - weights_ref[0] * total


def halo_part(side, nodes, weights, perm, orbitals, energies, sigma, halo):
    points = orbitals.shape[0]
    smem = pl.BlockSpec(memory_space=pltpu.SMEM)
    vmem = pl.BlockSpec(memory_space=pltpu.VMEM)
    return pl.pallas_call(
        halo_kernel,
        out_shape=pltpu.VMEM((1, ORBS), F32),
        in_specs=[smem] * 3 + [vmem] * 5,
        out_specs=vmem,
        scratch_shapes=[
            pltpu.VMEM((points, ORBS), BF16),
            pltpu.VMEM((2, points, ORBS), BF16),
        ],
        compiler_params=pltpu.CompilerParams(vmem_limit_bytes=16 << 20),
    )(
        side,
        nodes,
        weights,
        energies,
        pltpu.with_memory_space_constraint(sigma, pltpu.VMEM),
        pltpu.with_memory_space_constraint(perm, pltpu.VMEM),
        pltpu.with_memory_space_constraint(orbitals, pltpu.VMEM),
        pltpu.with_memory_space_constraint(halo, pltpu.VMEM),
    )


AXES = ("freq", "pts")


def device(f, p):
    return f * 16 + p


def inner_pairs():
    return [(device(f, p), device(f, p ^ 1)) for f in range(8) for p in range(16)]


def outer_pairs():
    pairs = []
    for f in range(8):
        for p in range(1, 15, 2):
            to = device(f ^ 4 if p == 7 else f, p + 1)
            pairs += [(device(f, p), to), (to, device(f, p))]
    return pairs


def total_over_devices(x):
    count = lax.axis_size(AXES)
    sent = jnp.broadcast_to(x, (count, ORBS))
    return jnp.sum(lax.all_to_all(sent, AXES, 0, 0, tiled=True), axis=0)


def body(orbitals, energies, freq_nodes, weights_q, screened, tile_rows, tile_cols, tile_count):
    position = lax.axis_index("pts")
    outer = lax.ppermute(orbitals, AXES, outer_pairs())
    inner = lax.ppermute(orbitals, AXES, inner_pairs())
    energies = energies[None, :]
    sigma, perm, halo = own_part(
        tile_count, tile_rows, tile_cols, freq_nodes, weights_q, orbitals, energies, screened
    )
    odd = (position % 2).astype(jnp.int32)
    for side, points in ((1 - odd, inner), (odd, outer)):
        sigma = halo_part(
            side[None], freq_nodes, weights_q, perm, points, energies, sigma, halo
        )
    return total_over_devices(sigma)


def solution(mesh):
    placed = (
        P("pts", None),
        P(),
        P("freq"),
        P("freq"),
        P("pts", "freq", None),
        P("pts"),
        P("pts"),
        P("pts"),
    )
    return jax.shard_map(body, mesh=mesh, in_specs=placed, out_specs=P(), check_vma=False)
```

```python
import functools

import jax
import jax.numpy as jnp
from jax import lax
from jax.experimental import pallas as pl
from jax.experimental.pallas import tpu as pltpu
from jax.sharding import PartitionSpec as P

ORBS = 512
TILE = 64
HALF = 32
BAND = 16
BLOCK = 4
SPAN = BLOCK * TILE
BLOCKS = BAND // BLOCK
UNROLL = 4
CHUNK = 64

F32 = jnp.float32
BF16 = jnp.bfloat16


def weight_row(energies, node):
    return energies / (energies * energies + node * node)


def block_terms(rows, cols_scaled, cols, w_of, ratio):
    dims = (((1,), (1,)), ((), ()))
    g0 = lax.dot_general(rows, cols_scaled(0), dims, preferred_element_type=F32)
    g1 = lax.dot_general(rows, cols_scaled(1), dims, preferred_element_type=F32)
    product = g0 * w_of(0).astype(F32) + ratio * (g1 * w_of(1).astype(F32))
    image = jnp.dot(product.astype(BF16), cols(), preferred_element_type=F32)
    return jnp.sum(image * rows.astype(F32), axis=0, keepdims=True)


def own_kernel(
    count_ref,
    energies_in,
    nodes_in,
    weights_in,
    slot_rows,
    slot_cols,
    orb_ref,
    screened_ref,
    sigma_ref,
    small,
    perm,
    halo,
    points,
    raw,
    dense,
    own_w,
    scaled,
    wide,
    energies_ref,
    nodes_ref,
    weights_ref,
    rows_ref,
    cols_ref,
    raw_sem,
    orb_sem,
    index_sem,
):
    slots = screened_ref.shape[0]
    chunks = slots // CHUNK
    count = count_ref[0]
    first = (lax.axis_index("pts") - 1) * BAND

    def fetch(k):
        part = pl.ds(k * CHUNK, CHUNK)
        return pltpu.make_async_copy(screened_ref.at[part], raw.at[part], raw_sem.at[k])

    bring = pltpu.make_async_copy(orb_ref, points, orb_sem)
    bring.start()
    pairs = (
        (energies_in, energies_ref),
        (nodes_in, nodes_ref),
        (weights_in, weights_ref),
        (slot_rows, rows_ref),
        (slot_cols, cols_ref),
    )
    index = [
        pltpu.make_async_copy(source, to, index_sem.at[k]) for k, (source, to) in enumerate(pairs)
    ]
    for copy in index:
        copy.start()
    for k in range(chunks):

        @pl.when(k * CHUNK < count)
        def _():
            fetch(k).start()

    for b in range(BLOCKS):

        def clear(r, carry):
            for c in range(b * BLOCK, b * BLOCK + 2 * BAND + BLOCK):
                dense[r, c] = jnp.zeros(dense.shape[2:], F32)
            return carry

        lax.fori_loop(b * BLOCK, (b + 1) * BLOCK, clear, 0)
    for copy in index:
        copy.wait()
    for f in range(2):
        small[f : f + 1] = weight_row(energies_ref[...], nodes_ref[f])
    ratio = weights_ref[1] / weights_ref[0]
    small[2:3] = jnp.full((1, ORBS), ratio, F32)
    small[3:4] = jnp.full((1, ORBS), -weights_ref[0], F32)
    bring.wait()

    for q in range(ORBS // 128):
        lanes = pl.ds(q * 128, 128)
        values = points[:, lanes].astype(F32)
        wide[q] = values
        for f in range(2):
            scaled[f, :, lanes] = (values * small[f : f + 1, lanes]).astype(BF16)
        for b in range(BLOCKS):
            for h in range(2):
                part = wide[q, pl.ds(b * SPAN + h, SPAN // 2, stride=2), :]
                perm[pl.ds(b * SPAN + h * SPAN // 2, SPAN // 2), lanes] = part.astype(BF16)

    def place(s):
        return rows_ref[s], cols_ref[s] - first

    def scatter(s, carry):
        r, c = place(s)
        dense[r, c] = dense[r, c] + raw[s].astype(F32)
        return carry

    for k in range(chunks):

        @pl.when(k * CHUNK < count)
        def _():
            fetch(k).wait()
            here = jnp.minimum(count - k * CHUNK, CHUNK)

            def several(i, carry):
                for d in range(UNROLL):
                    scatter(k * CHUNK + i * UNROLL + d, 0)
                return carry

            whole = here // UNROLL
            lax.fori_loop(0, whole, several, 0)
            lax.fori_loop(k * CHUNK + whole * UNROLL, k * CHUNK + here, scatter, 0)

    low = lax.broadcasted_iota(jnp.int32, (SPAN // 2, 2 * TILE), 1) < TILE

    def arrange(side, f, b, pair):
        to_b = BLOCKS - 1 - b if side == 0 else b
        to_pair = (BLOCKS - 1 - pair // 2) * 2 + pair % 2 if side == 0 else pair
        parts = []
        for d in range(2):
            c = side * BAND + 2 * pair + d
            parts.append(dense[pl.ds(b * BLOCK, BLOCK), c, f, :].reshape(SPAN // 2, 2 * TILE))
        v0, v1 = parts
        crossed = pltpu.roll(jnp.where(low, v1, v0), TILE, 1)
        even = jnp.where(low, v0, crossed)
        odd = jnp.where(low, crossed, v1)
        lanes = pl.ds(to_pair * 2 * TILE, 2 * TILE)
        to = own_w.at[f] if side == 1 else halo.at[side // 2, f]
        to[pl.ds(to_b * SPAN, SPAN // 2), lanes] = even.astype(BF16)
        to[pl.ds(to_b * SPAN + SPAN // 2, SPAN // 2), lanes] = odd.astype(BF16)

    def arrange_block(side, b, c):
        for f in range(2):
            for pair in range(2 * c, 2 * c + 2):
                arrange(side, f, b, pair)

    for b in range(BLOCKS):
        for c in range(BLOCKS):
            if c >= b:
                arrange_block(0, b, c)
            if c <= b:
                arrange_block(2, b, c)
    total = jnp.zeros((1, ORBS), F32)
    for b in range(BLOCKS):
        for c in range(BLOCKS):
            arrange_block(1, b, c)
        total += block_terms(
            perm[pl.ds(b * SPAN, SPAN), :],
            lambda f: scaled[f],
            lambda: points[...],
            lambda f: own_w[f, pl.ds(b * SPAN, SPAN), :],
            ratio,
        )
    sigma_ref[...] = -weights_ref[0] * total


def in_vmem(x):
    return pltpu.with_memory_space_constraint(x, pltpu.VMEM)


def own_part(count, energies, nodes, weights, rows, cols, orbitals, screened):
    points = orbitals.shape[0]
    smem = pl.BlockSpec(memory_space=pltpu.SMEM)
    vmem = pl.BlockSpec(memory_space=pltpu.VMEM)
    hbm = pl.BlockSpec(memory_space=pl.ANY)
    return pl.pallas_call(
        own_kernel,
        out_shape=(
            pltpu.VMEM((1, ORBS), F32),
            pltpu.VMEM((8, ORBS), F32),
            pltpu.VMEM((points, ORBS), BF16),
            pltpu.VMEM((2, 2, points, points), BF16),
        ),
        in_specs=[smem] + [hbm] * 7,
        out_specs=(vmem,) * 4,
        scratch_shapes=[
            pltpu.VMEM((points, ORBS), BF16),
            pltpu.VMEM(screened.shape, BF16),
            pltpu.VMEM((BAND, 3 * BAND, 2, TILE * TILE), F32),
            pltpu.VMEM((2, points, points), BF16),
            pltpu.VMEM((2, points, ORBS), BF16),
            pltpu.VMEM((ORBS // 128, points, 128), F32),
            pltpu.VMEM(energies.shape, F32),
            pltpu.SMEM(nodes.shape, F32),
            pltpu.SMEM(weights.shape, F32),
            pltpu.SMEM(rows.shape, jnp.int32),
            pltpu.SMEM(cols.shape, jnp.int32),
            pltpu.SemaphoreType.DMA((screened.shape[0] // CHUNK,)),
            pltpu.SemaphoreType.DMA,
            pltpu.SemaphoreType.DMA((5,)),
        ],
        compiler_params=pltpu.CompilerParams(vmem_limit_bytes=46 << 20),
    )(
        count,
        energies,
        nodes,
        weights,
        rows,
        cols,
        orbitals,
        screened,
    )


def halo_kernel(
    inner,
    small,
    sigma_in,
    perm_ref,
    orb_ref,
    halo_ref,
    sigma_ref,
    points,
    scaled,
):
    odd = lax.rem(lax.axis_index("pts"), 2)
    side = 1 - odd if inner else odd
    ratio = small[2:3, 0:1]
    total = jnp.zeros((1, ORBS), F32)
    for u in range(BLOCKS):
        block = (1 - side) * (BLOCKS - 1 - u) + side * u
        from_rows = pl.ds(pl.multiple_of(block * SPAN, SPAN), SPAN)
        rows = pl.ds(u * SPAN, SPAN)
        cols = pl.ds(0, (u + 1) * SPAN)
        points[rows, :] = orb_ref[from_rows, :]
        for f in range(2):
            scaled[f, rows] = (points[rows, :].astype(F32) * small[f : f + 1]).astype(BF16)
        total += block_terms(
            perm_ref[from_rows, :],
            lambda f: scaled[f, cols, :],
            lambda: points[cols, :],
            lambda f: halo_ref[side, f, rows, cols],
            ratio,
        )
    sigma_ref[...] = sigma_in[...] + small[3:4] * total


def halo_part(inner, small, sigma, perm, orbitals, halo):
    vmem = pl.BlockSpec(memory_space=pltpu.VMEM)
    held = (small, sigma, perm, orbitals, halo)
    return pl.pallas_call(
        functools.partial(halo_kernel, inner),
        out_shape=pltpu.VMEM((1, ORBS), F32),
        in_specs=[vmem] * len(held),
        out_specs=vmem,
        scratch_shapes=[
            pltpu.VMEM(orbitals.shape, BF16),
            pltpu.VMEM((2,) + orbitals.shape, BF16),
        ],
        compiler_params=pltpu.CompilerParams(vmem_limit_bytes=16 << 20),
    )(*(in_vmem(x) for x in held))


AXES = ("freq", "pts")


def device(f, p):
    return f * 16 + p


def inner_pairs():
    return [(device(f, p), device(f, p ^ 1)) for f in range(8) for p in range(16)]


def outer_pairs():
    pairs = []
    for f in range(8):
        for p in range(1, 15, 2):
            to = device(f ^ 4 if p == 7 else f, p + 1)
            pairs += [(device(f, p), to), (to, device(f, p))]
    return pairs


def total_over_devices(x):
    count = lax.axis_size(AXES)
    sent = jnp.broadcast_to(x, (count, ORBS))
    return jnp.sum(lax.all_to_all(sent, AXES, 0, 0, tiled=True), axis=0)


def body(orbitals, energies, freq_nodes, weights_q, screened, tile_rows, tile_cols, tile_count):
    outer = lax.ppermute(orbitals, AXES, outer_pairs())
    inner = lax.ppermute(orbitals, AXES, inner_pairs())
    sigma, small, perm, halo = own_part(
        tile_count,
        energies[None, :],
        freq_nodes,
        weights_q,
        tile_rows,
        tile_cols,
        orbitals,
        screened,
    )
    sigma = halo_part(True, small, sigma, perm, inner, halo)
    sigma = halo_part(False, small, sigma, perm, outer, halo)
    return total_over_devices(sigma)


def solution(mesh):
    placed = (
        P("pts", None),
        P(),
        P("freq"),
        P("freq"),
        P("pts", "freq", None),
        P("pts"),
        P("pts"),
        P("pts"),
    )
    return jax.shard_map(body, mesh=mesh, in_specs=placed, out_specs=P(), check_vma=False)
```

```python
import functools

import jax
import jax.numpy as jnp
from jax import lax
from jax.experimental import pallas as pl
from jax.experimental.pallas import tpu as pltpu
from jax.sharding import PartitionSpec as P

ORBS = 512
TILE = 64
HALF = 32
BAND = 16
BLOCK = 4
SPAN = BLOCK * TILE
BLOCKS = BAND // BLOCK
UNROLL = 4
CHUNK = 64

F32 = jnp.float32
BF16 = jnp.bfloat16


def weight_row(energies, node):
    return energies / (energies * energies + node * node)


def block_terms(rows, cols_scaled, cols, w_of, ratio):
    dims = (((1,), (1,)), ((), ()))
    g0 = lax.dot_general(rows, cols_scaled(0), dims, preferred_element_type=F32)
    g1 = lax.dot_general(rows, cols_scaled(1), dims, preferred_element_type=F32)
    product = g0 * w_of(0).astype(F32) + ratio * (g1 * w_of(1).astype(F32))
    image = jnp.dot(product.astype(BF16), cols(), preferred_element_type=F32)
    return jnp.sum(image * rows.astype(F32), axis=0, keepdims=True)


def own_kernel(
    count_in,
    energies_in,
    nodes_in,
    weights_in,
    slot_rows,
    slot_cols,
    orb_ref,
    screened_ref,
    sigma_ref,
    small,
    perm,
    halo,
    points,
    raw,
    dense,
    own_w,
    scaled,
    wide,
    energies_ref,
    nodes_ref,
    weights_ref,
    rows_ref,
    cols_ref,
    count_ref,
    raw_sem,
    early_sem,
):
    slots = screened_ref.shape[0]
    chunks = slots // CHUNK
    first = (lax.axis_index("pts") - 1) * BAND

    def fetch(k):
        part = pl.ds(k * CHUNK, CHUNK)
        return pltpu.make_async_copy(screened_ref.at[part], raw.at[part], raw_sem.at[k])

    pairs = (
        (count_in, count_ref),
        (energies_in, energies_ref),
        (nodes_in, nodes_ref),
        (weights_in, weights_ref),
        (slot_rows, rows_ref),
        (slot_cols, cols_ref),
        (orb_ref, points),
    )
    early = [
        pltpu.make_async_copy(source, to, early_sem.at[k]) for k, (source, to) in enumerate(pairs)
    ]
    for copy in early:
        copy.start()
    fetch(0).start()

    for b in range(BLOCKS):

        def clear(r, carry):
            for c in range(b * BLOCK, b * BLOCK + 2 * BAND + BLOCK):
                dense[r, c] = jnp.zeros(dense.shape[2:], F32)
            return carry

        lax.fori_loop(b * BLOCK, (b + 1) * BLOCK, clear, 0)
        if b == 0:
            early[0].wait()
            count = count_ref[0]
            for k in range(1, chunks):

                @pl.when(k * CHUNK < count)
                def _():
                    fetch(k).start()

    for copy in early[1:]:
        copy.wait()
    for f in range(2):
        small[f : f + 1] = weight_row(energies_ref[...], nodes_ref[f])
    ratio = weights_ref[1] / weights_ref[0]
    small[2:3] = jnp.full((1, ORBS), ratio, F32)
    small[3:4] = jnp.full((1, ORBS), -weights_ref[0], F32)

    for q in range(ORBS // 128):
        lanes = pl.ds(q * 128, 128)
        values = points[:, lanes].astype(F32)
        wide[q] = values
        for f in range(2):
            scaled[f, :, lanes] = (values * small[f : f + 1, lanes]).astype(BF16)
        for b in range(BLOCKS):
            for h in range(2):
                part = wide[q, pl.ds(b * SPAN + h, SPAN // 2, stride=2), :]
                perm[pl.ds(b * SPAN + h * SPAN // 2, SPAN // 2), lanes] = part.astype(BF16)

    def place(s):
        return rows_ref[s], cols_ref[s] - first

    def scatter(s, carry):
        r, c = place(s)
        dense[r, c] = dense[r, c] + raw[s].astype(F32)
        return carry

    fetch(0).wait()
    for k in range(chunks):

        @pl.when(k * CHUNK < count)
        def _():
            if k > 0:
                fetch(k).wait()
            here = jnp.minimum(count - k * CHUNK, CHUNK)

            def several(i, carry):
                for d in range(UNROLL):
                    scatter(k * CHUNK + i * UNROLL + d, 0)
                return carry

            whole = here // UNROLL
            lax.fori_loop(0, whole, several, 0)
            lax.fori_loop(k * CHUNK + whole * UNROLL, k * CHUNK + here, scatter, 0)

    low = lax.broadcasted_iota(jnp.int32, (SPAN // 2, 2 * TILE), 1) < TILE

    def arrange(side, f, b, pair):
        to_b = BLOCKS - 1 - b if side == 0 else b
        to_pair = (BLOCKS - 1 - pair // 2) * 2 + pair % 2 if side == 0 else pair
        parts = []
        for d in range(2):
            c = side * BAND + 2 * pair + d
            parts.append(dense[pl.ds(b * BLOCK, BLOCK), c, f, :].reshape(SPAN // 2, 2 * TILE))
        v0, v1 = parts
        crossed = pltpu.roll(jnp.where(low, v1, v0), TILE, 1)
        even = jnp.where(low, v0, crossed)
        odd = jnp.where(low, crossed, v1)
        lanes = pl.ds(to_pair * 2 * TILE, 2 * TILE)
        to = own_w.at[f] if side == 1 else halo.at[side // 2, f]
        to[pl.ds(to_b * SPAN, SPAN // 2), lanes] = even.astype(BF16)
        to[pl.ds(to_b * SPAN + SPAN // 2, SPAN // 2), lanes] = odd.astype(BF16)

    def arrange_block(side, b, c):
        for f in range(2):
            for pair in range(2 * c, 2 * c + 2):
                arrange(side, f, b, pair)

    for b in range(BLOCKS):
        for c in range(BLOCKS):
            if c >= b:
                arrange_block(0, b, c)
            if c <= b:
                arrange_block(2, b, c)
    total = jnp.zeros((1, ORBS), F32)
    for b in range(BLOCKS):
        for c in range(BLOCKS):
            arrange_block(1, b, c)
        total += block_terms(
            perm[pl.ds(b * SPAN, SPAN), :],
            lambda f: scaled[f],
            lambda: points[...],
            lambda f: own_w[f, pl.ds(b * SPAN, SPAN), :],
            ratio,
        )
    sigma_ref[...] = -weights_ref[0] * total


def in_vmem(x):
    return pltpu.with_memory_space_constraint(x, pltpu.VMEM)


def own_part(count, energies, nodes, weights, rows, cols, orbitals, screened):
    points = orbitals.shape[0]
    vmem = pl.BlockSpec(memory_space=pltpu.VMEM)
    hbm = pl.BlockSpec(memory_space=pl.ANY)
    return pl.pallas_call(
        own_kernel,
        out_shape=(
            pltpu.VMEM((1, ORBS), F32),
            pltpu.VMEM((8, ORBS), F32),
            pltpu.VMEM((points, ORBS), BF16),
            pltpu.VMEM((2, 2, points, points), BF16),
        ),
        in_specs=[hbm] * 8,
        out_specs=(vmem,) * 4,
        scratch_shapes=[
            pltpu.VMEM((points, ORBS), BF16),
            pltpu.VMEM(screened.shape, BF16),
            pltpu.VMEM((BAND, 3 * BAND, 2, TILE * TILE), F32),
            pltpu.VMEM((2, points, points), BF16),
            pltpu.VMEM((2, points, ORBS), BF16),
            pltpu.VMEM((ORBS // 128, points, 128), F32),
            pltpu.VMEM(energies.shape, F32),
            pltpu.SMEM(nodes.shape, F32),
            pltpu.SMEM(weights.shape, F32),
            pltpu.SMEM(rows.shape, jnp.int32),
            pltpu.SMEM(cols.shape, jnp.int32),
            pltpu.SMEM(count.shape, jnp.int32),
            pltpu.SemaphoreType.DMA((screened.shape[0] // CHUNK,)),
            pltpu.SemaphoreType.DMA((7,)),
        ],
        compiler_params=pltpu.CompilerParams(vmem_limit_bytes=46 << 20),
    )(
        count,
        energies,
        nodes,
        weights,
        rows,
        cols,
        orbitals,
        screened,
    )


def halo_kernel(
    inner,
    small,
    sigma_in,
    perm_ref,
    orb_ref,
    halo_ref,
    sigma_ref,
    points,
    scaled,
):
    odd = lax.rem(lax.axis_index("pts"), 2)
    side = 1 - odd if inner else odd
    ratio = small[2:3, 0:1]
    total = jnp.zeros((1, ORBS), F32)
    for u in range(BLOCKS):
        block = (1 - side) * (BLOCKS - 1 - u) + side * u
        from_rows = pl.ds(pl.multiple_of(block * SPAN, SPAN), SPAN)
        rows = pl.ds(u * SPAN, SPAN)
        cols = pl.ds(0, (u + 1) * SPAN)
        points[rows, :] = orb_ref[from_rows, :]
        for f in range(2):
            scaled[f, rows] = (points[rows, :].astype(F32) * small[f : f + 1]).astype(BF16)
        total += block_terms(
            perm_ref[from_rows, :],
            lambda f: scaled[f, cols, :],
            lambda: points[cols, :],
            lambda f: halo_ref[side, f, rows, cols],
            ratio,
        )
    sigma_ref[...] = sigma_in[...] + small[3:4] * total


def halo_part(inner, small, sigma, perm, orbitals, halo):
    vmem = pl.BlockSpec(memory_space=pltpu.VMEM)
    held = (small, sigma, perm, orbitals, halo)
    return pl.pallas_call(
        functools.partial(halo_kernel, inner),
        out_shape=pltpu.VMEM((1, ORBS), F32),
        in_specs=[vmem] * len(held),
        out_specs=vmem,
        scratch_shapes=[
            pltpu.VMEM(orbitals.shape, BF16),
            pltpu.VMEM((2,) + orbitals.shape, BF16),
        ],
        compiler_params=pltpu.CompilerParams(vmem_limit_bytes=16 << 20),
    )(*(in_vmem(x) for x in held))


AXES = ("freq", "pts")


def device(f, p):
    return f * 16 + p


def inner_pairs():
    return [(device(f, p), device(f, p ^ 1)) for f in range(8) for p in range(16)]


def outer_pairs():
    pairs = []
    for f in range(8):
        for p in range(1, 15, 2):
            to = device(f ^ 4 if p == 7 else f, p + 1)
            pairs += [(device(f, p), to), (to, device(f, p))]
    return pairs


def total_over_devices(x):
    count = lax.axis_size(AXES)
    sent = jnp.broadcast_to(x.astype(BF16).reshape(1, 4, ORBS // 4), (count, 4, ORBS // 4))
    return jnp.sum(lax.all_to_all(sent, AXES, 0, 0, tiled=True).astype(F32), axis=0).reshape(ORBS)


def body(orbitals, energies, freq_nodes, weights_q, screened, tile_rows, tile_cols, tile_count):
    outer = lax.ppermute(orbitals, AXES, outer_pairs())
    inner = lax.ppermute(orbitals, AXES, inner_pairs())
    sigma, small, perm, halo = own_part(
        tile_count,
        energies[None, :],
        freq_nodes,
        weights_q,
        tile_rows,
        tile_cols,
        orbitals,
        screened,
    )
    sigma = halo_part(True, small, sigma, perm, inner, halo)
    sigma = halo_part(False, small, sigma, perm, outer, halo)
    return total_over_devices(sigma)


def solution(mesh):
    placed = (
        P("pts", None),
        P(),
        P("freq"),
        P("freq"),
        P("pts", "freq", None),
        P("pts"),
        P("pts"),
        P("pts"),
    )
    return jax.shard_map(body, mesh=mesh, in_specs=placed, out_specs=P(), check_vma=False)
```
